512 devices in a mesh: snap: 8 (over x, core), space: 64 (over z, y).
Axes of the slice: x: 4, y: 8, z: 8, core: 2. Of those that a mesh axis runs over, the one named last changes fastest.
Arguments:
- velocity: float32 [2, 64, 2048, 1024], P(None, 'snap', 'space'), may hold values from -820 to 820
- metric_index: int32 [2048, 1024], P('space'), may hold values from 0 to 15
- metric_table: float32 [4, 16], replicated, may hold values from -2 to 2
Outputs:
- mode_field: float32 [63, 2048, 1024], P(None, 'space', 'snap')
- operator: float32 [63, 63], replicated
The draws below stay inside these ranges and needn't reach their ends.
All inputs are finite; a program needn't handle non-finite values.
Results may differ from the reference program's by a relative error of at most 0.00027.
Values sent between devices are 32-bit elements; how exact they have to be, the bound alone decides.
No kernel may reach another device: no remote copies, remote signals or barrier semaphores. Data moves between devices by JAX's collectives and lax.ppermute only.
A program may use at most 64 MiB of HBM per device.

```python
import math
import jax
import jax.numpy as jnp
from jax import lax

M = 64
KMET = 16
NETA = 1024
NXI = 2048
NCELLS = 2097152


def draw_velocity(key, part):
    key_noise = jax.random.fold_in(key, 11)
    key_scale = jax.random.fold_in(key, 12)
    cell_scale = jnp.exp(jax.random.uniform(key_scale, (1, 1, NXI, NETA), dtype=jnp.float32) * math.log(10.0))
    fraction = jnp.arange(NXI, dtype=jnp.float32) / max(NXI - 1, 1)
    sample = jax.random.truncated_normal(key_noise, -4.0, 4.0, (2, M, NXI, NETA), dtype=jnp.float32)
    growth = 1.0 + 2.0 * fraction
    return (sample * cell_scale * growth[None, None, :, None]).astype(jnp.float32)


def set_ends(entries, stream_key, smallest, high):
    dims = entries.shape
    spot = [jax.random.randint(jax.random.fold_in(stream_key, axis), (), 0, dims[axis]) for axis in range(len(dims))]
    entries = entries.at[tuple(spot)].set(smallest)
    longest = dims.index(max(dims))
    spot[longest] = (spot[longest] + 1) % dims[longest]
    return entries.at[tuple(spot)].set(high)


def setup_inputs(seed: int = 0) -> dict:
    streams_of = jax.random.split(jax.random.key(seed), 4)
    return {
        "velocity": draw_velocity(jax.random.fold_in(streams_of[3], 71), 0),
        "metric_index": set_ends(jax.random.randint(streams_of[1], (NXI, NETA), 0, KMET), jax.random.fold_in(streams_of[1], 1), 0, KMET - 1).astype(jnp.int32),
        "metric_table": jnp.clip(jax.random.uniform(streams_of[2], (4, KMET), jnp.float32, -2.0, 2.0), -2.0, 2.0),
    }


def along_rows(padded, row_count):
    near_diff = padded[:, :, 4:4 + row_count, :] - padded[:, :, 2:2 + row_count, :]
    middle = padded[:, :, 5:5 + row_count, :] - padded[:, :, 1:1 + row_count, :]
    far_diff = padded[:, :, 6:6 + row_count, :] - padded[:, :, 0:row_count, :]
    return (45.0 * near_diff - 9.0 * middle + far_diff) / 60.0

def along_cycle(field):
    near_diff = jnp.roll(field, -1, axis=-1) - jnp.roll(field, 1, axis=-1)
    middle = jnp.roll(field, -2, axis=-1) - jnp.roll(field, 2, axis=-1)
    far_diff = jnp.roll(field, -3, axis=-1) - jnp.roll(field, 3, axis=-1)
    return (45.0 * near_diff - 9.0 * middle + far_diff) / 60.0

def metric_lookup(metric_table, metric_index):
    classes = metric_table.shape[1]
    onehot = (metric_index[None, :, :] == jnp.arange(classes, dtype=jnp.int32)[:, None, None]).astype(jnp.float32)
    return jnp.einsum('ck,kxy->cxy', metric_table, onehot, precision=lax.Precision.HIGHEST)

def vorticity_of(velocity, padded, metric):
    row_count = velocity.shape[2]
    row_derivs = along_rows(padded, row_count)
    cycle_derivs = along_cycle(velocity)
    return metric[0] * row_derivs[1] + metric[1] * cycle_derivs[1] - metric[2] * row_derivs[0] - metric[3] * cycle_derivs[0]

def reference(velocity, metric_index, metric_table):
    metric = metric_lookup(metric_table, metric_index)

    def one_snapshot(position):
        snapshot = lax.dynamic_slice_in_dim(velocity, position, 1, 1)
        padded = jnp.pad(snapshot, ((0, 0), (0, 0), (3, 3), (0, 0)))
        return vorticity_of(snapshot, padded, metric)[0]
    vorticity = lax.map(one_snapshot, jnp.arange(M, dtype=jnp.int32))
    snapshot_rows = vorticity.reshape(M, NCELLS)
    gram = jnp.dot(snapshot_rows, snapshot_rows.T, precision=lax.Precision.HIGHEST) * (1.0 / NCELLS)
    factor = jnp.linalg.cholesky(gram).T
    leading = factor[:M - 1, :M - 1]
    coupling = factor[:M - 1, 1:]
    operator = jax.scipy.linalg.solve_triangular(leading, coupling.T, trans='T', lower=False).T
    mode_rows = jax.scipy.linalg.solve_triangular(leading, snapshot_rows[1:], trans='T', lower=False)
    return (mode_rows.reshape(M - 1, NXI, NETA), operator)
```

```python
import functools

import jax
import jax.numpy as jnp
from jax import lax
from jax.experimental import pallas as pl
from jax.experimental.pallas import tpu as pltpu
from jax.sharding import PartitionSpec as P

F32 = jnp.float32
BF16 = jnp.bfloat16
VMEM = pl.BlockSpec(memory_space=pltpu.VMEM)
SMEM = pl.BlockSpec(memory_space=pltpu.SMEM)
ANY = pl.BlockSpec(memory_space=pl.ANY)
MIB = 1024 * 1024


def params(mib):
    return pltpu.CompilerParams(vmem_limit_bytes=mib * MIB)


def cost(flops, nbytes):
    return pl.CostEstimate(flops=flops, bytes_accessed=nbytes, transcendentals=0)


def edges_kernel(vel, first_ref, last_ref, head, tail, sems):
    snaps, rows = vel.shape[1], vel.shape[2]
    copies = []
    for c in range(2):
        for side, (buf, start) in enumerate(((head, 0), (tail, rows - 8))):
            src = vel.at[c, :, pl.ds(start, 8), :]
            copies.append(pltpu.make_async_copy(src, buf.at[c], sems.at[2 * c + side]))
    for copy in copies:
        copy.start()
    for c in range(2):
        for side, (buf, out) in enumerate(((head, first_ref), (tail, last_ref))):
            copies[2 * c + side].wait()
            for r in range(3):
                row = r if side == 0 else 5 + r
                for m in range(snaps):
                    out[c, r, m : m + 1, :] = buf[c, m, row : row + 1, :]


def edges(velocity):
    _, snaps, _, cols = velocity.shape
    out = jax.ShapeDtypeStruct((2, 3, snaps, cols), F32)
    return pl.pallas_call(
        edges_kernel,
        out_shape=(out, out),
        in_specs=[ANY],
        out_specs=(VMEM, VMEM),
        scratch_shapes=[
            pltpu.VMEM((2, snaps, 8, cols), F32),
            pltpu.VMEM((2, snaps, 8, cols), F32),
            pltpu.SemaphoreType.DMA((4,)),
        ],
        compiler_params=params(8),
        name="edges",
    )(velocity)


def stencil(near, middle, far):
    return 45.0 * near - 9.0 * middle + far


def vorticity_kernel(table, vel, index_ref, out_ref, edge_ref, pad, metric, sems):
    snaps, rows, cols = vel.shape[1], vel.shape[2], vel.shape[3]
    blocks = cols // 128

    def copy(c, m):
        return pltpu.make_async_copy(vel.at[c, m], pad.at[c, m, pl.ds(8, rows), :], sems.at[c, m])

    for m in range(snaps):
        for c in range(2):
            copy(c, m).start()
    zero = jnp.zeros((2, snaps, 8, cols), F32)
    pad[:, :, 0:8, :] = zero
    pad[:, :, rows + 8 : rows + 16, :] = zero
    for r in range(rows // 8):
        index = index_ref[8 * r : 8 * r + 8, :]
        bits = [(index & (1 << b)) != 0 for b in range(4)]
        for t in range(4):
            level = [table[t, k] * (1.0 / 60.0) for k in range(16)]
            for bit in bits:
                level = [
                    jnp.where(bit, level[2 * k + 1], level[2 * k]) for k in range(len(level) // 2)
                ]
            metric[t, 8 * r : 8 * r + 8, :] = level[0]
    for t, slot in ((0, 0), (2, 1)):
        edge_ref[slot, 0:8, :] = metric[t, 0:8, :]
        edge_ref[slot, 8:16, :] = metric[t, rows - 8 : rows, :]

    def snapshot(m, carry):
        for c in range(2):
            copy(c, m).wait()
        for r in range(rows // 8):
            top = 8 + 8 * r
            total = None
            for c, xi_term, eta_term, sign in ((1, 0, 1, 1.0), (0, 2, 3, -1.0)):
                span = slice(8 * r, 8 * r + 8)

                def layer(k):
                    return pad[c, m, pl.ds(top + k, 8), :]

                along = stencil(
                    layer(1) - layer(-1), layer(2) - layer(-2), layer(3) - layer(-3)
                )
                field = layer(0)

                def turned(k):
                    return pltpu.roll(field, (-k) % cols, 1)

                around = stencil(
                    turned(1) - turned(-1), turned(2) - turned(-2), turned(3) - turned(-3)
                )
                term = metric[xi_term, span, :] * along + metric[eta_term, span, :] * around
                total = term if total is None else total - term
            for p in range(blocks):
                row = pl.multiple_of(m * rows + 8 * r, 8)
                out_ref[p, pl.ds(row, 8), :] = total[:, 128 * p : 128 * p + 128]
        return carry

    lax.fori_loop(0, snaps, snapshot, 0)


def vorticity_inside(table, velocity, index):
    _, snaps, rows, cols = velocity.shape
    return pl.pallas_call(
        vorticity_kernel,
        out_shape=(
            jax.ShapeDtypeStruct((cols // 128, snaps * rows, 128), F32),
            jax.ShapeDtypeStruct((2, 16, cols), F32),
        ),
        in_specs=[SMEM, ANY, VMEM],
        out_specs=(VMEM, VMEM),
        scratch_shapes=[
            pltpu.VMEM((2, snaps, rows + 16, cols), F32),
            pltpu.VMEM((4, rows, cols), F32),
            pltpu.SemaphoreType.DMA((2, snaps)),
        ],
        compiler_params=params(24),
        cost_estimate=cost(4000000000, 4 * MIB),
        name="vorticity_inside",
    )(table, velocity, index)


def border_kernel(part_ref, before, after, edge, out_ref):
    snaps, cols = before.shape[2], before.shape[3]
    rows = part_ref.shape[1] // snaps
    weights = ((-1.0, 9.0, -45.0), (0.0, -1.0, 9.0), (0.0, 0.0, -1.0))
    out_ref[...] = part_ref[...]
    for side in range(2):
        for r in range(3):
            halo = before if side == 0 else after
            row = r if side == 0 else rows - 1 - r
            line = r if side == 0 else 15 - r
            terms = []
            for c in (1, 0):
                total = None
                for k in range(3):
                    w = weights[r][k]
                    if w != 0.0:
                        near = halo[c, k] if side == 0 else halo[c, 2 - k]
                        piece = (w if side == 0 else -w) * near
                        total = piece if total is None else total + piece
                terms.append(total)
            added = edge[0, line : line + 1, :] * terms[0] - edge[1, line : line + 1, :] * terms[1]
            for p in range(cols // 128):
                place = pl.ds(row, snaps, stride=rows)
                out_ref[p, place, :] = part_ref[p, place, :] + added[:, 128 * p : 128 * p + 128]


def with_border(part, before, after, edge):
    return pl.pallas_call(
        border_kernel,
        out_shape=jax.ShapeDtypeStruct(part.shape, F32),
        in_specs=[VMEM] * 4,
        out_specs=VMEM,
        compiler_params=params(8),
        cost_estimate=cost(1000000, MIB // 2),
        name="border",
    )(part, before, after, edge)


def split3(value):
    high = value.astype(BF16)
    rest = value - high.astype(F32)
    middle = rest.astype(BF16)
    low = (rest - middle.astype(F32)).astype(BF16)
    return high, middle, low


def gram_kernel(scale, copies, z_ref, parts_ref, gram_ref):
    snaps = parts_ref.shape[0] // 3
    rows = z_ref.shape[0] // snaps
    total = None
    for i in range(0, rows, 2):
        for k in range(2):
            for part, value in enumerate(split3(z_ref[pl.ds(i + k, snaps, stride=rows), :])):
                at = (i + k) * 128
                parts_ref[part * snaps : (part + 1) * snaps, at : at + 128] = value
        both = parts_ref[:, i * 128 : i * 128 + 256]
        dims = (((1,), (1,)), ((), ()))
        piece = lax.dot_general(both, both, dims, preferred_element_type=F32)
        total = piece if total is None else total + piece
    cut = [slice(snaps * k, snaps * (k + 1)) for k in range(3)]
    order = ((2, 2), (1, 2), (2, 1), (0, 2), (2, 0), (1, 1), (0, 1), (1, 0), (0, 0))
    gram = None
    for a, b in order:
        block = total[cut[a], cut[b]]
        gram = block if gram is None else gram + block
    gram = gram * scale
    half = snaps // 2
    packed = jnp.concatenate([gram[:half], gram[half:]], axis=1)
    for n in range(copies):
        gram_ref[n] = packed


def gram_of(z, snaps, scale, copies):
    cells = z.shape[0] // snaps * 128
    return pl.pallas_call(
        functools.partial(gram_kernel, scale, copies),
        out_shape=(
            jax.ShapeDtypeStruct((3 * snaps, cells), BF16),
            jax.ShapeDtypeStruct((copies, snaps // 2, 2 * snaps), F32),
        ),
        in_specs=[VMEM],
        out_specs=(VMEM, VMEM),
        compiler_params=params(16),
        name="gram",
    )(z)


def added(values):
    total = values[0]
    for n in range(1, values.shape[0]):
        total = total + values[n]
    return total


def sum_kernel(in_ref, out_ref):
    total = added(in_ref)
    for n in range(out_ref.shape[0]):
        out_ref[n] = total


def summed(arrived, copies):
    return pl.pallas_call(
        sum_kernel,
        out_shape=jax.ShapeDtypeStruct((copies,) + arrived.shape[1:], F32),
        in_specs=[VMEM],
        out_specs=VMEM,
        compiler_params=params(4),
        name="summed",
    )(arrived)


def eliminate(rows):
    count = len(rows)
    sub = lax.broadcasted_iota(jnp.int32, (8, 128), 0)
    for b in range(count):
        cols = {
            v: [jnp.broadcast_to(rows[v][:, 8 * b + j : 8 * b + j + 1], (8, 128)) for j in range(8)]
            for v in range(b, count)
        }
        pivots = None
        for j in range(8):
            pivot = jnp.broadcast_to(cols[b][j][j : j + 1, :], (8, 128))
            pivots = pivot if pivots is None else jnp.where(sub == j, pivot, pivots)
            inverse = 1.0 / pivot
            lead = [jnp.broadcast_to(cols[b][jj][j : j + 1, :], (8, 128)) for jj in range(8)]
            lead_row = jnp.broadcast_to(rows[b][j : j + 1, :], (8, 128))
            for v in range(b, count):
                factor = cols[v][j] * inverse
                if v == b:
                    factor = jnp.where(sub > j, factor, 0.0)
                for jj in range(j + 1, 8):
                    cols[v][jj] = cols[v][jj] - factor * lead[jj]
                rows[v] = rows[v] - factor * lead_row
        root = lax.rsqrt(pivots)
        root = root * (1.5 - 0.5 * pivots * root * root)
        rows[b] = rows[b] * root
    return rows


def modes_kernel(sum_ref, parts_ref, mode_ref, operator_ref):
    half = sum_ref.shape[1]
    snaps = 2 * half
    less = snaps - 1
    packed = added(sum_ref)
    lane = lax.broadcasted_iota(jnp.int32, (8, 128), 1)
    sub = lax.broadcasted_iota(jnp.int32, (8, 128), 0)
    rows = []
    for v in range(snaps // 8):
        if v < half // 8:
            block = packed[8 * v : 8 * v + 8]
        else:
            block = pltpu.roll(packed[8 * v - half : 8 * v - half + 8], 128 - snaps, 1)
        one = jnp.where(lane == snaps + 8 * v + sub, 1.0, 0.0)
        rows.append(jnp.where(lane < snaps, block, one))
    rows = eliminate(rows)
    couple, inverse, left = [], [], []
    for v in range(snaps // 8):
        upper = jnp.where((lane < snaps) & (lane < 8 * v + sub), 0.0, rows[v])
        turned = pltpu.roll(upper, 127, 1)
        couple.append(jnp.where(lane < less, turned, 0.0)[:, :snaps])
        turned = pltpu.roll(rows[v], 128 - snaps, 1)
        inverse.append(jnp.where(lane < less, turned, 0.0)[:, :snaps])
        turned = pltpu.roll(rows[v], 128 - snaps + 1, 1)
        left.append(jnp.where((lane > 0) & (lane < snaps), turned, 0.0)[:, :snaps])
    parts = split3(jnp.concatenate(left, axis=0))
    wide = jnp.concatenate([jnp.concatenate([part] * 3, axis=1) for part in parts], axis=0)
    for i in range(0, parts_ref.shape[1] // 128, 2):
        product = jnp.dot(wide, parts_ref[:, i * 128 : i * 128 + 256], preferred_element_type=F32)
        result = product[2 * snaps :] + product[snaps : 2 * snaps] + product[:snaps]
        for k in range(2):
            place = pl.ds(i + k, less, stride=mode_ref.shape[0] // less)
            mode_ref[place, :] = result[:less, 128 * k : 128 * k + 128]
    operator = lax.dot_general(
        jnp.concatenate(couple, axis=0),
        jnp.concatenate(inverse, axis=0),
        (((1,), (1,)), ((), ())),
        precision=lax.Precision.HIGHEST,
        preferred_element_type=F32,
    )
    operator_ref[...] = operator[:less, :less]


def modes_of(arrived, parts):
    snaps = 2 * arrived.shape[1]
    rows = parts.shape[1] // 128
    return pl.pallas_call(
        modes_kernel,
        out_shape=(
            jax.ShapeDtypeStruct(((snaps - 1) * rows, 128), F32),
            jax.ShapeDtypeStruct((snaps - 1, snaps - 1), F32),
        ),
        in_specs=[VMEM, VMEM],
        out_specs=(VMEM, VMEM),
        compiler_params=params(16),
        name="modes",
    )(arrived, parts)


def space_groups(size):
    if size <= 8:
        return [None]
    inner = 8
    near = [[a * inner + b for b in range(inner)] for a in range(size // inner)]
    far = [[a * inner + b for a in range(size // inner)] for b in range(inner)]
    return [near, far]


def local(velocity, index, table):
    size, snap_devices = lax.axis_size("space"), lax.axis_size("snap")
    _, snaps, rows, cols = velocity.shape
    first, last = edges(velocity)
    up = [(i, i + 1) for i in range(size - 1)]
    down = [(i + 1, i) for i in range(size - 1)]
    before = lax.ppermute(last, "space", up)
    after = lax.ppermute(first, "space", down)
    part, edge = vorticity_inside(table, velocity, index)
    whole = with_border(part, before, after, edge)
    owned = lax.all_to_all(whole, "snap", 0, 0)
    all_snaps = snaps * snap_devices
    z = owned.reshape(all_snaps * rows, 128)
    scale = 1.0 / (rows * size * cols)
    stages = [("snap", None, snap_devices)]
    for groups in space_groups(size):
        stages.append(("space", groups, size if groups is None else len(groups[0])))
    parts, sent = gram_of(z, all_snaps, scale, stages[0][2])
    for n, (axis, groups, _) in enumerate(stages):
        arrived = lax.all_to_all(sent, axis, 0, 0, axis_index_groups=groups)
        if n + 1 < len(stages):
            sent = summed(arrived, stages[n + 1][2])
    mode, operator = modes_of(arrived, parts)
    return mode.reshape(all_snaps - 1, rows, 128), operator


def solution(mesh):
    in_specs = (P(None, "snap", "space", None), P("space", None), P())
    out_specs = (P(None, "space", "snap"), P())
    return jax.shard_map(local, mesh=mesh, in_specs=in_specs, out_specs=out_specs, check_vma=False)
```

```python
import functools

import jax
import jax.numpy as jnp
from jax import lax
from jax.experimental import pallas as pl
from jax.experimental.pallas import tpu as pltpu
from jax.sharding import PartitionSpec as P

F32 = jnp.float32
BF16 = jnp.bfloat16
VMEM = pl.BlockSpec(memory_space=pltpu.VMEM)
SMEM = pl.BlockSpec(memory_space=pltpu.SMEM)
HBM = pl.BlockSpec(memory_space=pltpu.HBM)
MIB = 1024 * 1024


def params(mib):
    return pltpu.CompilerParams(vmem_limit_bytes=mib * MIB)


def cost(flops, nbytes):
    return pl.CostEstimate(flops=flops, bytes_accessed=nbytes, transcendentals=0)


def edges_kernel(vel, first_ref, last_ref, head, tail, sems):
    snaps, rows = vel.shape[1], vel.shape[2]
    copies = []
    for c in range(2):
        for side, (buf, start) in enumerate(((head, 0), (tail, rows - 8))):
            src = vel.at[c, :, pl.ds(start, 8), :]
            copies.append(pltpu.make_async_copy(src, buf.at[c], sems.at[2 * c + side]))
    for copy in copies:
        copy.start()
    for c in range(2):
        for side, (buf, out) in enumerate(((head, first_ref), (tail, last_ref))):
            copies[2 * c + side].wait()
            for r in range(3):
                row = r if side == 0 else 5 + r
                for m in range(snaps):
                    out[c, r, m : m + 1, :] = buf[c, m, row : row + 1, :]


def edges(velocity):
    _, snaps, _, cols = velocity.shape
    out = jax.ShapeDtypeStruct((2, 3, snaps, cols), F32)
    return pl.pallas_call(
        edges_kernel,
        out_shape=(out, out),
        in_specs=[HBM],
        out_specs=(VMEM, VMEM),
        scratch_shapes=[
            pltpu.VMEM((2, snaps, 8, cols), F32),
            pltpu.VMEM((2, snaps, 8, cols), F32),
            pltpu.SemaphoreType.DMA((4,)),
        ],
        compiler_params=params(52),
        name="edges",
    )(velocity)


def stencil(near, middle, far):
    return 45.0 * near - 9.0 * middle + far


def metric_of(table, index):
    bits = [(index & (1 << b)) != 0 for b in range(4)]
    terms = []
    for t in range(4):
        level = [table[t, k] * (1.0 / 60.0) for k in range(16)]
        for bit in bits:
            level = [jnp.where(bit, level[2 * k + 1], level[2 * k]) for k in range(len(level) // 2)]
        terms.append(level[0])
    return terms


def vorticity_kernel(table, vel, index_hbm, out_ref, edge_ref, raw, lines, index_ref, sems, index_sem):
    rows, cols = index_hbm.shape
    snaps, blocks = vel.shape[1] // rows, cols // 128
    lane = lax.broadcasted_iota(jnp.int32, (8, 128), 1)
    copies = {}
    for p in range(blocks):
        for c in range(2):
            src = vel.at[c, :, pl.ds(128 * p, 128)]
            copies[c, p] = pltpu.make_async_copy(src, raw.at[c, p], sems.at[c, p])
            copies[c, p].start()
    index_copy = pltpu.make_async_copy(index_hbm, index_ref, index_sem)
    index_copy.start()
    zero = jnp.zeros((2, 3, snaps, cols), F32)
    lines[:, 0:3] = zero
    lines[:, rows + 3 : rows + 6] = zero
    for p in range(blocks):
        for c in range(2):
            copies[c, p].wait()
            for i in range(rows):
                tile = raw[c, p, pl.ds(i, snaps, stride=rows), :]
                lines[c, i + 3, :, 128 * p : 128 * p + 128] = tile

    index_copy.wait()

    def band(r, carry):
        top = pl.multiple_of(8 * r, 8)
        metric = []
        for p in range(blocks):
            index = index_ref[pl.ds(top, 8), 128 * p : 128 * p + 128]
            metric.append(metric_of(table, index))

        for s in range(8):
            i = top + s + 3
            total = [None] * blocks
            for c, xi_term, eta_term in ((1, 0, 1), (0, 2, 3)):
                field = [lines[c, i, :, 128 * p : 128 * p + 128] for p in range(blocks)]
                left = {k: [pltpu.roll(f, 128 - k, 1) for f in field] for k in (1, 2, 3)}
                right = {k: [pltpu.roll(f, k, 1) for f in field] for k in (1, 2, 3)}
                for p in range(blocks):
                    span = slice(128 * p, 128 * p + 128)
                    along = stencil(
                        lines[c, i + 1, :, span] - lines[c, i - 1, :, span],
                        lines[c, i + 2, :, span] - lines[c, i - 2, :, span],
                        lines[c, i + 3, :, span] - lines[c, i - 3, :, span],
                    )
                    diffs = []
                    for k in (1, 2, 3):
                        ahead = jnp.where(
                            lane < 128 - k, left[k][p], left[k][(p + 1) % blocks]
                        )
                        behind = jnp.where(lane >= k, right[k][p], right[k][(p - 1) % blocks])
                        diffs.append(ahead - behind)
                    around = stencil(*diffs)
                    term = (
                        metric[p][xi_term][s : s + 1] * along
                        + metric[p][eta_term][s : s + 1] * around
                    )
                    total[p] = term if total[p] is None else total[p] - term
            for p in range(blocks):
                out_ref[p, top + s] = total[p]

        for slot, t in ((0, 0), (1, 2)):
            for p in range(blocks):
                edge_ref[slot, pl.ds(top, 8), 128 * p : 128 * p + 128] = metric[p][t]
        return carry

    lax.fori_loop(0, rows // 8, band, 0)


def vorticity_inside(table, velocity, index):
    _, snaps, rows, cols = velocity.shape
    flat = velocity.reshape(2, snaps * rows, cols)
    return pl.pallas_call(
        vorticity_kernel,
        out_shape=(
            jax.ShapeDtypeStruct((cols // 128, rows, snaps, 128), F32),
            jax.ShapeDtypeStruct((2, rows, cols), F32),
        ),
        in_specs=[SMEM, HBM, HBM],
        out_specs=(VMEM, VMEM),
        scratch_shapes=[
            pltpu.VMEM((2, cols // 128, snaps * rows, 128), F32),
            pltpu.VMEM((2, rows + 6, snaps, cols), F32),
            pltpu.VMEM((rows, cols), jnp.int32),
            pltpu.SemaphoreType.DMA((2, cols // 128)),
            pltpu.SemaphoreType.DMA,
        ],
        compiler_params=params(52),
        cost_estimate=cost(4000000000, 4 * MIB),
        name="vorticity_inside",
    )(table, flat, index)


def border_kernel(part_ref, before, after, edge, out_ref):
    rows, cols = part_ref.shape[1], before.shape[3]
    weights = ((-1.0, 9.0, -45.0), (0.0, -1.0, 9.0), (0.0, 0.0, -1.0))
    out_ref[:, 3 : rows - 3] = part_ref[:, 3 : rows - 3]
    for side in range(2):
        for r in range(3):
            halo = before if side == 0 else after
            row = r if side == 0 else rows - 1 - r
            terms = []
            for c in (1, 0):
                total = None
                for k in range(3):
                    w = weights[r][k]
                    if w != 0.0:
                        near = halo[c, k] if side == 0 else halo[c, 2 - k]
                        piece = (w if side == 0 else -w) * near
                        total = piece if total is None else total + piece
                terms.append(total)
            more = edge[0, row : row + 1, :] * terms[0] - edge[1, row : row + 1, :] * terms[1]
            for p in range(cols // 128):
                out_ref[p, row] = part_ref[p, row] + more[:, 128 * p : 128 * p + 128]


def with_border(part, before, after, edge):
    return pl.pallas_call(
        border_kernel,
        out_shape=jax.ShapeDtypeStruct(part.shape, F32),
        in_specs=[VMEM] * 4,
        out_specs=VMEM,
        compiler_params=params(8),
        cost_estimate=cost(1000000, MIB // 2),
        name="border",
    )(part, before, after, edge)


def split3(value):
    high = value.astype(BF16)
    rest = value - high.astype(F32)
    middle = rest.astype(BF16)
    low = (rest - middle.astype(F32)).astype(BF16)
    return high, middle, low


def gram_kernel(scale, copies, z_ref, parts_ref, gram_ref):
    snaps, rows = parts_ref.shape[0] // 3, z_ref.shape[1]
    total = None
    for i in range(0, rows, 2):
        for k in range(2):
            for part, value in enumerate(split3(z_ref[:, i + k].reshape(snaps, 128))):
                at = (i + k) * 128
                parts_ref[part * snaps : (part + 1) * snaps, at : at + 128] = value
        both = parts_ref[:, i * 128 : i * 128 + 256]
        dims = (((1,), (1,)), ((), ()))
        piece = lax.dot_general(both, both, dims, preferred_element_type=F32)
        total = piece if total is None else total + piece
    cut = [slice(snaps * k, snaps * (k + 1)) for k in range(3)]
    order = ((2, 2), (1, 2), (2, 1), (0, 2), (2, 0), (1, 1), (0, 1), (1, 0), (0, 0))
    gram = None
    for a, b in order:
        block = total[cut[a], cut[b]]
        gram = block if gram is None else gram + block
    gram = gram * scale
    half = snaps // 2
    packed = jnp.concatenate([gram[:half], gram[half:]], axis=1)
    for n in range(copies):
        gram_ref[n] = packed


def gram_of(z, scale, copies):
    snaps, cells = z.shape[0] * z.shape[2], z.shape[1] * z.shape[3]
    return pl.pallas_call(
        functools.partial(gram_kernel, scale, copies),
        out_shape=(
            jax.ShapeDtypeStruct((3 * snaps, cells), BF16),
            jax.ShapeDtypeStruct((copies, snaps // 2, 2 * snaps), F32),
        ),
        in_specs=[VMEM],
        out_specs=(VMEM, VMEM),
        compiler_params=params(16),
        name="gram",
    )(z)


def added(values):
    total = values[0]
    for n in range(1, values.shape[0]):
        total = total + values[n]
    return total


def sum_kernel(in_ref, out_ref):
    total = added(in_ref)
    for n in range(out_ref.shape[0]):
        out_ref[n] = total


def summed(arrived, copies):
    return pl.pallas_call(
        sum_kernel,
        out_shape=jax.ShapeDtypeStruct((copies,) + arrived.shape[1:], F32),
        in_specs=[VMEM],
        out_specs=VMEM,
        compiler_params=params(4),
        name="summed",
    )(arrived)


def eliminate(rows):
    count = len(rows)
    sub = lax.broadcasted_iota(jnp.int32, (8, 128), 0)
    for b in range(count):
        cols = {
            v: [jnp.broadcast_to(rows[v][:, 8 * b + j : 8 * b + j + 1], (8, 128)) for j in range(8)]
            for v in range(b, count)
        }
        pivots = None
        for j in range(8):
            pivot = jnp.broadcast_to(cols[b][j][j : j + 1, :], (8, 128))
            pivots = pivot if pivots is None else jnp.where(sub == j, pivot, pivots)
            inverse = 1.0 / pivot
            lead = [jnp.broadcast_to(cols[b][jj][j : j + 1, :], (8, 128)) for jj in range(8)]
            lead_row = jnp.broadcast_to(rows[b][j : j + 1, :], (8, 128))
            for v in range(b, count):
                factor = cols[v][j] * inverse
                if v == b:
                    factor = jnp.where(sub > j, factor, 0.0)
                for jj in range(j + 1, 8):
                    cols[v][jj] = cols[v][jj] - factor * lead[jj]
                rows[v] = rows[v] - factor * lead_row
        root = lax.rsqrt(pivots)
        root = root * (1.5 - 0.5 * pivots * root * root)
        rows[b] = rows[b] * root
    return rows


def modes_kernel(sum_ref, parts_ref, mode_ref, operator_ref):
    half = sum_ref.shape[1]
    snaps = 2 * half
    less = snaps - 1
    packed = added(sum_ref)
    lane = lax.broadcasted_iota(jnp.int32, (8, 128), 1)
    sub = lax.broadcasted_iota(jnp.int32, (8, 128), 0)
    rows = []
    for v in range(snaps // 8):
        if v < half // 8:
            block = packed[8 * v : 8 * v + 8]
        else:
            block = pltpu.roll(packed[8 * v - half : 8 * v - half + 8], 128 - snaps, 1)
        one = jnp.where(lane == snaps + 8 * v + sub, 1.0, 0.0)
        rows.append(jnp.where(lane < snaps, block, one))
    rows = eliminate(rows)
    couple, inverse, left = [], [], []
    for v in range(snaps // 8):
        upper = jnp.where((lane < snaps) & (lane < 8 * v + sub), 0.0, rows[v])
        turned = pltpu.roll(upper, 127, 1)
        couple.append(jnp.where(lane < less, turned, 0.0)[:, :snaps])
        turned = pltpu.roll(rows[v], 128 - snaps, 1)
        inverse.append(jnp.where(lane < less, turned, 0.0)[:, :snaps])
        turned = pltpu.roll(rows[v], 128 - snaps + 1, 1)
        left.append(jnp.where((lane > 0) & (lane < snaps), turned, 0.0)[:, :snaps])
    parts = split3(jnp.concatenate(left, axis=0))
    wide = jnp.concatenate([jnp.concatenate([part] * 3, axis=1) for part in parts], axis=0)
    for i in range(0, parts_ref.shape[1] // 128, 2):
        product = jnp.dot(wide, parts_ref[:, i * 128 : i * 128 + 256], preferred_element_type=F32)
        result = product[2 * snaps :] + product[snaps : 2 * snaps] + product[:snaps]
        for k in range(2):
            place = pl.ds(i + k, less, stride=mode_ref.shape[0] // less)
            mode_ref[place, :] = result[:less, 128 * k : 128 * k + 128]
    operator = lax.dot_general(
        jnp.concatenate(couple, axis=0),
        jnp.concatenate(inverse, axis=0),
        (((1,), (1,)), ((), ())),
        precision=lax.Precision.HIGHEST,
        preferred_element_type=F32,
    )
    operator_ref[...] = operator[:less, :less]


def modes_of(arrived, parts):
    snaps = 2 * arrived.shape[1]
    rows = parts.shape[1] // 128
    return pl.pallas_call(
        modes_kernel,
        out_shape=(
            jax.ShapeDtypeStruct(((snaps - 1) * rows, 128), F32),
            jax.ShapeDtypeStruct((snaps - 1, snaps - 1), F32),
        ),
        in_specs=[VMEM, VMEM],
        out_specs=(VMEM, VMEM),
        compiler_params=params(16),
        name="modes",
    )(arrived, parts)


def space_groups(size):
    if size <= 8:
        return [None]
    inner = 8
    near = [[a * inner + b for b in range(inner)] for a in range(size // inner)]
    far = [[a * inner + b for a in range(size // inner)] for b in range(inner)]
    return [near, far]


def local(velocity, index, table):
    size, snap_devices = lax.axis_size("space"), lax.axis_size("snap")
    _, snaps, rows, cols = velocity.shape
    first, last = edges(velocity)
    up = [(i, i + 1) for i in range(size - 1)]
    down = [(i + 1, i) for i in range(size - 1)]
    before = lax.ppermute(last, "space", up)
    after = lax.ppermute(first, "space", down)
    part, edge = vorticity_inside(table, velocity, index)
    whole = with_border(part, before, after, edge)
    owned = lax.all_to_all(whole, "snap", 0, 0)
    all_snaps = snaps * snap_devices
    scale = 1.0 / (rows * size * cols)
    stages = [("snap", None, snap_devices)]
    for groups in space_groups(size):
        stages.append(("space", groups, size if groups is None else len(groups[0])))
    parts, sent = gram_of(owned, scale, stages[0][2])
    for n, (axis, groups, _) in enumerate(stages):
        arrived = lax.all_to_all(sent, axis, 0, 0, axis_index_groups=groups)
        if n + 1 < len(stages):
            sent = summed(arrived, stages[n + 1][2])
    mode, operator = modes_of(arrived, parts)
    return mode.reshape(all_snaps - 1, rows, 128), operator


def solution(mesh):
    in_specs = (P(None, "snap", "space", None), P("space", None), P())
    out_specs = (P(None, "space", "snap"), P())
    return jax.shard_map(local, mesh=mesh, in_specs=in_specs, out_specs=out_specs, check_vma=False)
```

```python
import functools

import jax
import jax.numpy as jnp
from jax import lax
from jax.experimental import pallas as pl
from jax.experimental.pallas import tpu as pltpu
from jax.sharding import PartitionSpec as P

F32 = jnp.float32
BF16 = jnp.bfloat16
VMEM = pl.BlockSpec(memory_space=pltpu.VMEM)
SMEM = pl.BlockSpec(memory_space=pltpu.SMEM)
HBM = pl.BlockSpec(memory_space=pltpu.HBM)
MIB = 1024 * 1024


def params(mib):
    return pltpu.CompilerParams(vmem_limit_bytes=mib * MIB)


def cost(flops, nbytes):
    return pl.CostEstimate(flops=flops, bytes_accessed=nbytes, transcendentals=0)


def edges_kernel(vel, first_ref, last_ref, head, tail, sems):
    snaps, rows = vel.shape[1], vel.shape[2]
    copies = []
    for c in range(2):
        for side, (buf, start) in enumerate(((head, 0), (tail, rows - 8))):
            src = vel.at[c, :, pl.ds(start, 8), :]
            copies.append(pltpu.make_async_copy(src, buf.at[c], sems.at[2 * c + side]))
    for copy in copies:
        copy.start()
    for c in range(2):
        for side, (buf, out) in enumerate(((head, first_ref), (tail, last_ref))):
            copies[2 * c + side].wait()
            for r in range(3):
                row = r if side == 0 else 5 + r
                for m in range(snaps):
                    out[c, r, m : m + 1, :] = buf[c, m, row : row + 1, :]


def edges(velocity):
    _, snaps, _, cols = velocity.shape
    out = jax.ShapeDtypeStruct((2, 3, snaps, cols), F32)
    return pl.pallas_call(
        edges_kernel,
        out_shape=(out, out),
        in_specs=[HBM],
        out_specs=(VMEM, VMEM),
        scratch_shapes=[
            pltpu.VMEM((2, snaps, 8, cols), F32),
            pltpu.VMEM((2, snaps, 8, cols), F32),
            pltpu.SemaphoreType.DMA((4,)),
        ],
        compiler_params=params(52),
        name="edges",
    )(velocity)


def stencil(near, middle, far):
    return 45.0 * near - 9.0 * middle + far


def metric_of(table, index):
    bits = [(index & (1 << b)) != 0 for b in range(4)]
    terms = []
    for t in range(4):
        level = [table[t, k] * (1.0 / 60.0) for k in range(16)]
        for bit in bits:
            level = [jnp.where(bit, level[2 * k + 1], level[2 * k]) for k in range(len(level) // 2)]
        terms.append(level[0])
    return terms


def band_of(line, metric, out_ref, out_first, blocks):
    lane = lax.broadcasted_iota(jnp.int32, (8, 128), 1)
    for s in range(8):
        total = [None] * blocks
        for c, xi_term, eta_term in ((1, 0, 1), (0, 2, 3)):
            field = [line(c, p, s) for p in range(blocks)]
            for p in range(blocks):
                span = slice(128 * p, 128 * p + 128)
                along = stencil(
                    line(c, p, s + 1) - line(c, p, s - 1),
                    line(c, p, s + 2) - line(c, p, s - 2),
                    line(c, p, s + 3) - line(c, p, s - 3),
                )
                after, before = field[(p + 1) % blocks], field[(p - 1) % blocks]
                diffs = []
                for k in (1, 2, 3):
                    ahead = pltpu.roll(jnp.where(lane < k, after, field[p]), 128 - k, 1)
                    behind = pltpu.roll(jnp.where(lane < 128 - k, field[p], before), k, 1)
                    diffs.append(ahead - behind)
                around = stencil(*diffs)
                term = (
                    metric[xi_term][s : s + 1, span] * along
                    + metric[eta_term][s : s + 1, span] * around
                )
                total[p] = term if total[p] is None else total[p] - term
        for p in range(blocks):
            out_ref[p, out_first + s] = total[p]


def vorticity_kernel(table, vel, index_ref, out_ref, edge_ref, lines):
    rows, cols = index_ref.shape
    snaps, blocks = vel.shape[1] // rows, cols // 128
    zero = jnp.zeros((2, blocks, 3 * snaps, 128), F32)
    lines[:, :, : 3 * snaps] = zero
    lines[:, :, (rows + 3) * snaps :] = zero
    for c in range(2):
        for m in range(snaps):
            for r in range(0, rows, 8):
                for p in range(blocks):
                    tile = vel[c, m * rows + r : m * rows + r + 8, 128 * p : 128 * p + 128]
                    lines[c, p, pl.ds((r + 3) * snaps + m, 8, stride=snaps), :] = tile

    def band(r, carry):
        top = pl.multiple_of(8 * r, 8)

        def line(c, p, s):
            return lines[c, p, pl.ds(pl.multiple_of((top + s + 3) * snaps, 8), snaps), :]

        metric = metric_of(table, index_ref[pl.ds(top, 8), :])
        edge_ref[0, pl.ds(top, 8), :] = metric[0]
        edge_ref[1, pl.ds(top, 8), :] = metric[2]
        band_of(line, metric, out_ref, top, blocks)
        return carry

    lax.fori_loop(0, rows // 8, band, 0)


def vorticity_inside(table, flat, index):
    rows, cols = index.shape
    snaps, blocks = flat.shape[1] // rows, cols // 128
    return pl.pallas_call(
        vorticity_kernel,
        out_shape=(
            jax.ShapeDtypeStruct((blocks, rows, snaps, 128), F32),
            jax.ShapeDtypeStruct((2, rows, cols), F32),
        ),
        in_specs=[SMEM, VMEM, VMEM],
        out_specs=(VMEM, VMEM),
        scratch_shapes=[pltpu.VMEM((2, blocks, (rows + 6) * snaps, 128), F32)],
        compiler_params=params(16),
        cost_estimate=cost(4000000000, 4 * MIB),
        name="vorticity_inside",
    )(table, flat, index)


def border_kernel(part_ref, before, after, edge, out_ref):
    rows, cols = part_ref.shape[1], before.shape[3]
    weights = ((-1.0, 9.0, -45.0), (0.0, -1.0, 9.0), (0.0, 0.0, -1.0))
    out_ref[:, 3 : rows - 3] = part_ref[:, 3 : rows - 3]
    for side in range(2):
        for r in range(3):
            halo = before if side == 0 else after
            row = r if side == 0 else rows - 1 - r
            terms = []
            for c in (1, 0):
                total = None
                for k in range(3):
                    w = weights[r][k]
                    if w != 0.0:
                        near = halo[c, k] if side == 0 else halo[c, 2 - k]
                        piece = (w if side == 0 else -w) * near
                        total = piece if total is None else total + piece
                terms.append(total)
            more = edge[0, row : row + 1, :] * terms[0] - edge[1, row : row + 1, :] * terms[1]
            for p in range(cols // 128):
                out_ref[p, row] = part_ref[p, row] + more[:, 128 * p : 128 * p + 128]


def with_border(part, before, after, edge):
    return pl.pallas_call(
        border_kernel,
        out_shape=jax.ShapeDtypeStruct(part.shape, F32),
        in_specs=[VMEM] * 4,
        out_specs=VMEM,
        compiler_params=params(8),
        cost_estimate=cost(1000000, MIB // 2),
        name="border",
    )(part, before, after, edge)


def split3(value):
    high = value.astype(BF16)
    rest = value - high.astype(F32)
    middle = rest.astype(BF16)
    low = (rest - middle.astype(F32)).astype(BF16)
    return high, middle, low


def gram_kernel(scale, copies, z_ref, parts_ref, gram_ref):
    snaps, rows = parts_ref.shape[0] // 3, z_ref.shape[1]
    total = None
    for i in range(0, rows, 2):
        for k in range(2):
            for part, value in enumerate(split3(z_ref[:, i + k].reshape(snaps, 128))):
                at = (i + k) * 128
                parts_ref[part * snaps : (part + 1) * snaps, at : at + 128] = value
        both = parts_ref[:, i * 128 : i * 128 + 256]
        dims = (((1,), (1,)), ((), ()))
        piece = lax.dot_general(both, both, dims, preferred_element_type=F32)
        total = piece if total is None else total + piece
    cut = [slice(snaps * k, snaps * (k + 1)) for k in range(3)]
    order = ((2, 2), (1, 2), (2, 1), (0, 2), (2, 0), (1, 1), (0, 1), (1, 0), (0, 0))
    gram = None
    for a, b in order:
        block = total[cut[a], cut[b]]
        gram = block if gram is None else gram + block
    gram = gram * scale
    half = snaps // 2
    packed = jnp.concatenate([gram[:half], gram[half:]], axis=1)
    for n in range(copies):
        gram_ref[n] = packed


def gram_of(z, scale, copies):
    snaps, cells = z.shape[0] * z.shape[2], z.shape[1] * z.shape[3]
    return pl.pallas_call(
        functools.partial(gram_kernel, scale, copies),
        out_shape=(
            jax.ShapeDtypeStruct((3 * snaps, cells), BF16),
            jax.ShapeDtypeStruct((copies, snaps // 2, 2 * snaps), F32),
        ),
        in_specs=[VMEM],
        out_specs=(VMEM, VMEM),
        compiler_params=params(16),
        name="gram",
    )(z)


def added(values):
    total = values[0]
    for n in range(1, values.shape[0]):
        total = total + values[n]
    return total


def sum_kernel(in_ref, out_ref):
    total = added(in_ref)
    for n in range(out_ref.shape[0]):
        out_ref[n] = total


def summed(arrived, copies):
    return pl.pallas_call(
        sum_kernel,
        out_shape=jax.ShapeDtypeStruct((copies,) + arrived.shape[1:], F32),
        in_specs=[VMEM],
        out_specs=VMEM,
        compiler_params=params(4),
        name="summed",
    )(arrived)


def eliminate(rows):
    count = len(rows)
    sub = lax.broadcasted_iota(jnp.int32, (8, 128), 0)
    for b in range(count):
        cols = {
            v: [jnp.broadcast_to(rows[v][:, 8 * b + j : 8 * b + j + 1], (8, 128)) for j in range(8)]
            for v in range(b, count)
        }
        pivots = None
        for j in range(8):
            pivot = jnp.broadcast_to(cols[b][j][j : j + 1, :], (8, 128))
            pivots = pivot if pivots is None else jnp.where(sub == j, pivot, pivots)
            inverse = 1.0 / pivot
            lead = [jnp.broadcast_to(cols[b][jj][j : j + 1, :], (8, 128)) for jj in range(8)]
            lead_row = jnp.broadcast_to(rows[b][j : j + 1, :], (8, 128))
            for v in range(b, count):
                factor = cols[v][j] * inverse
                if v == b:
                    factor = jnp.where(sub > j, factor, 0.0)
                for jj in range(j + 1, 8):
                    cols[v][jj] = cols[v][jj] - factor * lead[jj]
                rows[v] = rows[v] - factor * lead_row
        root = lax.rsqrt(pivots)
        root = root * (1.5 - 0.5 * pivots * root * root)
        rows[b] = rows[b] * root
    return rows


def modes_kernel(sum_ref, parts_ref, mode_ref, operator_ref):
    half = sum_ref.shape[1]
    snaps = 2 * half
    less = snaps - 1
    packed = added(sum_ref)
    lane = lax.broadcasted_iota(jnp.int32, (8, 128), 1)
    sub = lax.broadcasted_iota(jnp.int32, (8, 128), 0)
    rows = []
    for v in range(snaps // 8):
        if v < half // 8:
            block = packed[8 * v : 8 * v + 8]
        else:
            block = pltpu.roll(packed[8 * v - half : 8 * v - half + 8], 128 - snaps, 1)
        one = jnp.where(lane == snaps + 8 * v + sub, 1.0, 0.0)
        rows.append(jnp.where(lane < snaps, block, one))
    rows = eliminate(rows)
    couple, inverse, left = [], [], []
    for v in range(snaps // 8):
        upper = jnp.where((lane < snaps) & (lane < 8 * v + sub), 0.0, rows[v])
        turned = pltpu.roll(upper, 127, 1)
        couple.append(jnp.where(lane < less, turned, 0.0)[:, :snaps])
        turned = pltpu.roll(rows[v], 128 - snaps, 1)
        inverse.append(jnp.where(lane < less, turned, 0.0)[:, :snaps])
        turned = pltpu.roll(rows[v], 128 - snaps + 1, 1)
        left.append(jnp.where((lane > 0) & (lane < snaps), turned, 0.0)[:, :snaps])
    parts = split3(jnp.concatenate(left, axis=0))
    wide = jnp.concatenate([jnp.concatenate([part] * 3, axis=1) for part in parts], axis=0)
    for i in range(0, parts_ref.shape[1] // 128, 2):
        product = jnp.dot(wide, parts_ref[:, i * 128 : i * 128 + 256], preferred_element_type=F32)
        result = product[2 * snaps :] + product[snaps : 2 * snaps] + product[:snaps]
        for k in range(2):
            place = pl.ds(i + k, less, stride=mode_ref.shape[0] // less)
            mode_ref[place, :] = result[:less, 128 * k : 128 * k + 128]
    operator = lax.dot_general(
        jnp.concatenate(couple, axis=0),
        jnp.concatenate(inverse, axis=0),
        (((1,), (1,)), ((), ())),
        precision=lax.Precision.HIGHEST,
        preferred_element_type=F32,
    )
    operator_ref[...] = operator[:less, :less]


def modes_of(arrived, parts):
    snaps = 2 * arrived.shape[1]
    rows = parts.shape[1] // 128
    return pl.pallas_call(
        modes_kernel,
        out_shape=(
            jax.ShapeDtypeStruct(((snaps - 1) * rows, 128), F32),
            jax.ShapeDtypeStruct((snaps - 1, snaps - 1), F32),
        ),
        in_specs=[VMEM, VMEM],
        out_specs=(VMEM, VMEM),
        compiler_params=params(16),
        name="modes",
    )(arrived, parts)


def space_groups(size):
    if size <= 8:
        return [None]
    inner = 8
    near = [[a * inner + b for b in range(inner)] for a in range(size // inner)]
    far = [[a * inner + b for a in range(size // inner)] for b in range(inner)]
    return [near, far]


def local(velocity, index, table):
    size, snap_devices = lax.axis_size("space"), lax.axis_size("snap")
    _, snaps, rows, cols = velocity.shape
    first, last = edges(velocity)
    up = [(i, i + 1) for i in range(size - 1)]
    down = [(i + 1, i) for i in range(size - 1)]
    before = lax.ppermute(last, "space", up)
    after = lax.ppermute(first, "space", down)
    flat = velocity.reshape(2, snaps * rows, cols)
    part, edge = vorticity_inside(table, flat, index)
    whole = with_border(part, before, after, edge)
    owned = lax.all_to_all(whole, "snap", 0, 0)
    all_snaps = snaps * snap_devices
    scale = 1.0 / (rows * size * cols)
    stages = [("snap", None, snap_devices)]
    for groups in space_groups(size):
        stages.append(("space", groups, size if groups is None else len(groups[0])))
    parts, sent = gram_of(owned, scale, stages[0][2])
    for n, (axis, groups, _) in enumerate(stages):
        arrived = lax.all_to_all(sent, axis, 0, 0, axis_index_groups=groups)
        if n + 1 < len(stages):
            sent = summed(arrived, stages[n + 1][2])
    mode, operator = modes_of(arrived, parts)
    return mode.reshape(all_snaps - 1, rows, 128), operator


def solution(mesh):
    in_specs = (P(None, "snap", "space", None), P("space", None), P())
    out_specs = (P(None, "space", "snap"), P())
    return jax.shard_map(local, mesh=mesh, in_specs=in_specs, out_specs=out_specs, check_vma=False)
```

```python
import functools

import jax
import jax.numpy as jnp
from jax import lax
from jax.experimental import pallas as pl
from jax.experimental.pallas import tpu as pltpu
from jax.sharding import PartitionSpec as P

F32 = jnp.float32
BF16 = jnp.bfloat16
VMEM = pl.BlockSpec(memory_space=pltpu.VMEM)
SMEM = pl.BlockSpec(memory_space=pltpu.SMEM)
HBM = pl.BlockSpec(memory_space=pltpu.HBM)
MIB = 1024 * 1024


def params(mib):
    return pltpu.CompilerParams(vmem_limit_bytes=mib * MIB)


def cost(flops, nbytes):
    return pl.CostEstimate(flops=flops, bytes_accessed=nbytes, transcendentals=0)


def edges_kernel(vel, first_ref, last_ref, head, tail, sems):
    snaps, rows = vel.shape[1], vel.shape[2]
    copies = []
    for c in range(2):
        for side, (buf, start) in enumerate(((head, 0), (tail, rows - 8))):
            src = vel.at[c, :, pl.ds(start, 8), :]
            copies.append(pltpu.make_async_copy(src, buf.at[c], sems.at[2 * c + side]))
    for copy in copies:
        copy.start()
    for c in range(2):
        for side, (buf, out) in enumerate(((head, first_ref), (tail, last_ref))):
            copies[2 * c + side].wait()
            for r in range(3):
                row = r if side == 0 else 5 + r
                for m in range(snaps):
                    out[c, r, m : m + 1, :] = buf[c, m, row : row + 1, :]


def edges(velocity):
    _, snaps, _, cols = velocity.shape
    out = jax.ShapeDtypeStruct((2, 3, snaps, cols), F32)
    return pl.pallas_call(
        edges_kernel,
        out_shape=(out, out),
        in_specs=[HBM],
        out_specs=(VMEM, VMEM),
        scratch_shapes=[
            pltpu.VMEM((2, snaps, 8, cols), F32),
            pltpu.VMEM((2, snaps, 8, cols), F32),
            pltpu.SemaphoreType.DMA((4,)),
        ],
        compiler_params=params(52),
        name="edges",
    )(velocity)


def stencil(near, middle, far):
    return 45.0 * near - 9.0 * middle + far


def metric_of(table, index):
    bits = [(index & (1 << b)) != 0 for b in range(4)]
    terms = []
    for t in range(4):
        level = [table[t, k] * (1.0 / 60.0) for k in range(16)]
        for bit in bits:
            level = [jnp.where(bit, level[2 * k + 1], level[2 * k]) for k in range(len(level) // 2)]
        terms.append(level[0])
    return terms


def band_of(line, metric, out_ref, out_first, blocks):
    lane = lax.broadcasted_iota(jnp.int32, (8, 128), 1)
    for s in range(8):
        total = [None] * blocks
        for c, xi_term, eta_term in ((1, 0, 1), (0, 2, 3)):
            field = [line(c, p, s) for p in range(blocks)]
            for p in range(blocks):
                span = slice(128 * p, 128 * p + 128)
                along = stencil(
                    line(c, p, s + 1) - line(c, p, s - 1),
                    line(c, p, s + 2) - line(c, p, s - 2),
                    line(c, p, s + 3) - line(c, p, s - 3),
                )
                after, before = field[(p + 1) % blocks], field[(p - 1) % blocks]
                diffs = []
                for k in (1, 2, 3):
                    ahead = pltpu.roll(jnp.where(lane < k, after, field[p]), 128 - k, 1)
                    behind = pltpu.roll(jnp.where(lane < 128 - k, field[p], before), k, 1)
                    diffs.append(ahead - behind)
                around = stencil(*diffs)
                term = (
                    metric[xi_term][s : s + 1, span] * along
                    + metric[eta_term][s : s + 1, span] * around
                )
                total[p] = term if total[p] is None else total[p] - term
        for p in range(blocks):
            out_ref[p, out_first + s] = total[p]


def vorticity_kernel(table, vel, index_ref, out_ref, edge_ref, lines):
    rows, cols = index_ref.shape
    snaps, blocks = vel.shape[1] // rows, cols // 128
    zero = jnp.zeros((2, blocks, 3 * snaps, 128), F32)
    lines[:, :, : 3 * snaps] = zero
    lines[:, :, (rows + 3) * snaps :] = zero
    for c in range(2):
        for m in range(snaps):
            for r in range(0, rows, 8):
                for p in range(blocks):
                    tile = vel[c, m * rows + r : m * rows + r + 8, 128 * p : 128 * p + 128]
                    lines[c, p, pl.ds((r + 3) * snaps + m, 8, stride=snaps), :] = tile

    def band(r, carry):
        top = pl.multiple_of(8 * r, 8)

        def line(c, p, s):
            return lines[c, p, pl.ds(pl.multiple_of((top + s + 3) * snaps, 8), snaps), :]

        metric = metric_of(table, index_ref[pl.ds(top, 8), :])
        edge_ref[0, pl.ds(top, 8), :] = metric[0]
        edge_ref[1, pl.ds(top, 8), :] = metric[2]
        band_of(line, metric, out_ref, top, blocks)
        return carry

    lax.fori_loop(0, rows // 8, band, 0)


def vorticity_inside(table, flat, index):
    rows, cols = index.shape
    snaps, blocks = flat.shape[1] // rows, cols // 128
    return pl.pallas_call(
        vorticity_kernel,
        out_shape=(
            jax.ShapeDtypeStruct((blocks, rows, snaps, 128), F32),
            jax.ShapeDtypeStruct((2, rows, cols), F32),
        ),
        in_specs=[SMEM, VMEM, VMEM],
        out_specs=(VMEM, VMEM),
        scratch_shapes=[pltpu.VMEM((2, blocks, (rows + 6) * snaps, 128), F32)],
        compiler_params=params(16),
        cost_estimate=cost(4000000000, 4 * MIB),
        name="vorticity_inside",
    )(table, flat, index)


def border_kernel(part_ref, before, after, edge, out_ref):
    rows, cols = part_ref.shape[1], before.shape[3]
    weights = ((-1.0, 9.0, -45.0), (0.0, -1.0, 9.0), (0.0, 0.0, -1.0))
    out_ref[:, 3 : rows - 3] = part_ref[:, 3 : rows - 3]
    for side in range(2):
        for r in range(3):
            halo = before if side == 0 else after
            row = r if side == 0 else rows - 1 - r
            terms = []
            for c in (1, 0):
                total = None
                for k in range(3):
                    w = weights[r][k]
                    if w != 0.0:
                        near = halo[c, k] if side == 0 else halo[c, 2 - k]
                        piece = (w if side == 0 else -w) * near
                        total = piece if total is None else total + piece
                terms.append(total)
            more = edge[0, row : row + 1, :] * terms[0] - edge[1, row : row + 1, :] * terms[1]
            for p in range(cols // 128):
                out_ref[p, row] = part_ref[p, row] + more[:, 128 * p : 128 * p + 128]


def with_border(part, before, after, edge):
    return pl.pallas_call(
        border_kernel,
        out_shape=jax.ShapeDtypeStruct(part.shape, F32),
        in_specs=[VMEM] * 4,
        out_specs=VMEM,
        compiler_params=params(8),
        cost_estimate=cost(1000000, MIB // 2),
        name="border",
    )(part, before, after, edge)


def split3(value):
    high = value.astype(BF16)
    rest = value - high.astype(F32)
    middle = rest.astype(BF16)
    low = (rest - middle.astype(F32)).astype(BF16)
    return high, middle, low


def gram_kernel(scale, copies, z_ref, parts_ref, gram_ref):
    snaps, rows = parts_ref.shape[0] // 3, z_ref.shape[1]
    total = None
    for i in range(0, rows, 2):
        for k in range(2):
            for part, value in enumerate(split3(z_ref[:, i + k].reshape(snaps, 128))):
                at = (i + k) * 128
                parts_ref[part * snaps : (part + 1) * snaps, at : at + 128] = value
        both = parts_ref[:, i * 128 : i * 128 + 256]
        dims = (((1,), (1,)), ((), ()))
        piece = lax.dot_general(both, both, dims, preferred_element_type=F32)
        total = piece if total is None else total + piece
    cut = [slice(snaps * k, snaps * (k + 1)) for k in range(3)]
    order = ((2, 2), (1, 2), (2, 1), (0, 2), (2, 0), (1, 1), (0, 1), (1, 0), (0, 0))
    gram = None
    for a, b in order:
        block = total[cut[a], cut[b]]
        gram = block if gram is None else gram + block
    gram = gram * scale
    half = snaps // 2
    tiles = []
    for block in (gram[:half, :half], gram[:half, half:], gram[half:, half:]):
        pieces = [block[8 * k : 8 * k + 8] for k in range(half // 8)]
        tiles.append(jnp.concatenate(pieces, axis=1))
    packed = jnp.concatenate(tiles, axis=0)
    for n in range(copies):
        gram_ref[n] = packed


def gram_of(z, scale, copies):
    snaps, cells = z.shape[0] * z.shape[2], z.shape[1] * z.shape[3]
    return pl.pallas_call(
        functools.partial(gram_kernel, scale, copies),
        out_shape=(
            jax.ShapeDtypeStruct((3 * snaps, cells), BF16),
            jax.ShapeDtypeStruct((copies, 24, 128), F32),
        ),
        in_specs=[VMEM],
        out_specs=(VMEM, VMEM),
        compiler_params=params(16),
        name="gram",
    )(z)


def added(values):
    total = values[0]
    for n in range(1, values.shape[0]):
        total = total + values[n]
    return total


def sum_kernel(in_ref, out_ref):
    total = added(in_ref)
    for n in range(out_ref.shape[0]):
        out_ref[n] = total


def summed(arrived, copies):
    return pl.pallas_call(
        sum_kernel,
        out_shape=jax.ShapeDtypeStruct((copies,) + arrived.shape[1:], F32),
        in_specs=[VMEM],
        out_specs=VMEM,
        compiler_params=params(4),
        name="summed",
    )(arrived)


def eliminate(rows):
    count = len(rows)
    sub = lax.broadcasted_iota(jnp.int32, (8, 128), 0)
    for b in range(count):
        cols = {
            v: [jnp.broadcast_to(rows[v][:, 8 * b + j : 8 * b + j + 1], (8, 128)) for j in range(8)]
            for v in range(b, count)
        }
        pivots = None
        for j in range(8):
            pivot = jnp.broadcast_to(cols[b][j][j : j + 1, :], (8, 128))
            pivots = pivot if pivots is None else jnp.where(sub == j, pivot, pivots)
            inverse = 1.0 / pivot
            lead = [jnp.broadcast_to(cols[b][jj][j : j + 1, :], (8, 128)) for jj in range(8)]
            lead_row = jnp.broadcast_to(rows[b][j : j + 1, :], (8, 128))
            for v in range(b, count):
                factor = cols[v][j] * inverse
                if v == b:
                    factor = jnp.where(sub > j, factor, 0.0)
                for jj in range(j + 1, 8):
                    cols[v][jj] = cols[v][jj] - factor * lead[jj]
                rows[v] = rows[v] - factor * lead_row
        root = lax.rsqrt(pivots)
        root = root * (1.5 - 0.5 * pivots * root * root)
        rows[b] = rows[b] * root
    return rows


def modes_kernel(sum_ref, parts_ref, mode_ref, operator_ref):
    snaps = parts_ref.shape[0] // 3
    half, less = snaps // 2, snaps - 1
    packed = added(sum_ref)
    lane = lax.broadcasted_iota(jnp.int32, (8, 128), 1)
    sub = lax.broadcasted_iota(jnp.int32, (8, 128), 0)
    first, cross, last = packed[:8], packed[8:16], packed[16:]

    def piece(tile, k, at):
        turn = (at - half * k) % 128
        return pltpu.roll(tile, turn, 1) if turn else tile

    fill = jnp.zeros((128 - half, 128), F32)
    cross_rows = [piece(cross, k, 0) for k in range(half // 8)]
    crossed = jnp.concatenate(cross_rows + [fill], axis=0).T
    rows = []
    for v in range(snaps // 8):
        if v < half // 8:
            block = jnp.where(lane < half, piece(first, v, 0), piece(cross, v, half))
        else:
            k = v - half // 8
            block = jnp.where(lane < half, crossed[8 * k : 8 * k + 8], piece(last, k, half))
        one = jnp.where(lane == snaps + 8 * v + sub, 1.0, 0.0)
        rows.append(jnp.where(lane < snaps, block, one))
    rows = eliminate(rows)
    couple, inverse, left = [], [], []
    for v in range(snaps // 8):
        upper = jnp.where((lane < snaps) & (lane < 8 * v + sub), 0.0, rows[v])
        turned = pltpu.roll(upper, 127, 1)
        couple.append(jnp.where(lane < less, turned, 0.0)[:, :snaps])
        turned = pltpu.roll(rows[v], 128 - snaps, 1)
        inverse.append(jnp.where(lane < less, turned, 0.0)[:, :snaps])
        turned = pltpu.roll(rows[v], 128 - snaps + 1, 1)
        left.append(jnp.where((lane > 0) & (lane < snaps), turned, 0.0)[:, :snaps])
    parts = split3(jnp.concatenate(left, axis=0))
    wide = jnp.concatenate([jnp.concatenate([part] * 3, axis=1) for part in parts], axis=0)
    for i in range(0, parts_ref.shape[1] // 128, 2):
        product = jnp.dot(wide, parts_ref[:, i * 128 : i * 128 + 256], preferred_element_type=F32)
        result = product[2 * snaps :] + product[snaps : 2 * snaps] + product[:snaps]
        for k in range(2):
            place = pl.ds(i + k, less, stride=mode_ref.shape[0] // less)
            mode_ref[place, :] = result[:less, 128 * k : 128 * k + 128]
    operator = lax.dot_general(
        jnp.concatenate(couple, axis=0),
        jnp.concatenate(inverse, axis=0),
        (((1,), (1,)), ((), ())),
        precision=lax.Precision.HIGHEST,
        preferred_element_type=F32,
    )
    operator_ref[...] = operator[:less, :less]


def modes_of(arrived, parts):
    snaps, rows = parts.shape[0] // 3, parts.shape[1] // 128
    return pl.pallas_call(
        modes_kernel,
        out_shape=(
            jax.ShapeDtypeStruct(((snaps - 1) * rows, 128), F32),
            jax.ShapeDtypeStruct((snaps - 1, snaps - 1), F32),
        ),
        in_specs=[VMEM, VMEM],
        out_specs=(VMEM, VMEM),
        compiler_params=params(16),
        name="modes",
    )(arrived, parts)


def space_groups(size):
    if size <= 8:
        return [None]
    inner = 8
    near = [[a * inner + b for b in range(inner)] for a in range(size // inner)]
    far = [[a * inner + b for a in range(size // inner)] for b in range(inner)]
    return [near, far]


def local(velocity, index, table):
    size, snap_devices = lax.axis_size("space"), lax.axis_size("snap")
    _, snaps, rows, cols = velocity.shape
    first, last = edges(velocity)
    up = [(i, i + 1) for i in range(size - 1)]
    down = [(i + 1, i) for i in range(size - 1)]
    before = lax.ppermute(last, "space", up)
    after = lax.ppermute(first, "space", down)
    flat = velocity.reshape(2, snaps * rows, cols)
    part, edge = vorticity_inside(table, flat, index)
    whole = with_border(part, before, after, edge)
    owned = lax.all_to_all(whole, "snap", 0, 0)
    all_snaps = snaps * snap_devices
    scale = 1.0 / (rows * size * cols)
    stages = [("snap", None, snap_devices)]
    for groups in space_groups(size):
        stages.append(("space", groups, size if groups is None else len(groups[0])))
    parts, sent = gram_of(owned, scale, stages[0][2])
    for n, (axis, groups, _) in enumerate(stages):
        arrived = lax.all_to_all(sent, axis, 0, 0, axis_index_groups=groups)
        if n + 1 < len(stages):
            sent = summed(arrived, stages[n + 1][2])
    mode, operator = modes_of(arrived, parts)
    return mode.reshape(all_snaps - 1, rows, 128), operator


def solution(mesh):
    in_specs = (P(None, "snap", "space", None), P("space", None), P())
    out_specs = (P(None, "space", "snap"), P())
    return jax.shard_map(local, mesh=mesh, in_specs=in_specs, out_specs=out_specs, check_vma=False)
```

```python
import functools

import jax
import jax.numpy as jnp
from jax import lax
from jax.experimental import pallas as pl
from jax.experimental.pallas import tpu as pltpu
from jax.sharding import PartitionSpec as P

F32 = jnp.float32
BF16 = jnp.bfloat16
VMEM = pl.BlockSpec(memory_space=pltpu.VMEM)
SMEM = pl.BlockSpec(memory_space=pltpu.SMEM)
HBM = pl.BlockSpec(memory_space=pltpu.HBM)
MIB = 1024 * 1024


def params(mib):
    return pltpu.CompilerParams(vmem_limit_bytes=mib * MIB)


def cost(flops, nbytes):
    return pl.CostEstimate(flops=flops, bytes_accessed=nbytes, transcendentals=0)


def edges_kernel(vel, first_ref, last_ref, head, tail, sems):
    snaps, rows = vel.shape[1], vel.shape[2]
    copies = []
    for c in range(2):
        for side, (buf, start) in enumerate(((head, 0), (tail, rows - 8))):
            src = vel.at[c, :, pl.ds(start, 8), :]
            copies.append(pltpu.make_async_copy(src, buf.at[c], sems.at[2 * c + side]))
    for copy in copies:
        copy.start()
    for c in range(2):
        for side, (buf, out) in enumerate(((head, first_ref), (tail, last_ref))):
            copies[2 * c + side].wait()
            for r in range(3):
                row = r if side == 0 else 5 + r
                for m in range(snaps):
                    out[c, r, m : m + 1, :] = buf[c, m, row : row + 1, :]


def edges(velocity):
    _, snaps, _, cols = velocity.shape
    out = jax.ShapeDtypeStruct((2, 3, snaps, cols), F32)
    return pl.pallas_call(
        edges_kernel,
        out_shape=(out, out),
        in_specs=[HBM],
        out_specs=(VMEM, VMEM),
        scratch_shapes=[
            pltpu.VMEM((2, snaps, 8, cols), F32),
            pltpu.VMEM((2, snaps, 8, cols), F32),
            pltpu.SemaphoreType.DMA((4,)),
        ],
        compiler_params=params(52),
        name="edges",
    )(velocity)


def stencil(near, middle, far):
    return 45.0 * near - 9.0 * middle + far


def metric_of(table, index):
    bits = [(index & (1 << b)) != 0 for b in range(4)]
    terms = []
    for t in range(4):
        level = [table[t, k] * (1.0 / 60.0) for k in range(16)]
        for bit in bits:
            level = [jnp.where(bit, level[2 * k + 1], level[2 * k]) for k in range(len(level) // 2)]
        terms.append(level[0])
    return terms


def band_of(line, metric, out_ref, out_first, blocks):
    lane = lax.broadcasted_iota(jnp.int32, (8, 128), 1)
    for p in range(blocks):
        span = slice(128 * p, 128 * p + 128)
        window = [[line(c, p, s) for s in range(-3, 11)] for c in range(2)]
        for s in range(8):
            total = None
            for c, xi_term, eta_term in ((1, 0, 1), (0, 2, 3)):
                near = window[c][s : s + 7]
                along = stencil(near[4] - near[2], near[5] - near[1], near[6] - near[0])
                here = near[3]
                after, before = line(c, (p + 1) % blocks, s), line(c, (p - 1) % blocks, s)
                diffs = []
                for k in (1, 2, 3):
                    ahead = pltpu.roll(jnp.where(lane < k, after, here), 128 - k, 1)
                    behind = pltpu.roll(jnp.where(lane < 128 - k, here, before), k, 1)
                    diffs.append(ahead - behind)
                around = stencil(*diffs)
                term = (
                    metric[xi_term][s : s + 1, span] * along
                    + metric[eta_term][s : s + 1, span] * around
                )
                total = term if total is None else total - term
            out_ref[p, out_first + s] = total


def vorticity_kernel(table, vel, index_ref, out_ref, edge_ref, lines):
    rows, cols = index_ref.shape
    snaps, blocks = vel.shape[1] // rows, cols // 128
    zero = jnp.zeros((2, blocks, 3 * snaps, 128), F32)
    lines[:, :, : 3 * snaps] = zero
    lines[:, :, (rows + 3) * snaps :] = zero
    for c in range(2):
        for m in range(snaps):
            for r in range(0, rows, 8):
                for p in range(blocks):
                    tile = vel[c, m * rows + r : m * rows + r + 8, 128 * p : 128 * p + 128]
                    lines[c, p, pl.ds((r + 3) * snaps + m, 8, stride=snaps), :] = tile

    def band(r, carry):
        top = 8 * r

        def line(c, p, s):
            return lines[c, p, pl.ds((top + s + 3) * snaps, snaps), :]

        metric = metric_of(table, index_ref[pl.ds(top, 8), :])
        edge_ref[0, pl.ds(top, 8), :] = metric[0]
        edge_ref[1, pl.ds(top, 8), :] = metric[2]
        band_of(line, metric, out_ref, top, blocks)
        return carry

    for r in range(rows // 8):
        band(r, 0)


def vorticity_inside(table, flat, index):
    rows, cols = index.shape
    snaps, blocks = flat.shape[1] // rows, cols // 128
    return pl.pallas_call(
        vorticity_kernel,
        out_shape=(
            jax.ShapeDtypeStruct((blocks, rows, snaps, 128), F32),
            jax.ShapeDtypeStruct((2, rows, cols), F32),
        ),
        in_specs=[SMEM, VMEM, VMEM],
        out_specs=(VMEM, VMEM),
        scratch_shapes=[pltpu.VMEM((2, blocks, (rows + 6) * snaps, 128), F32)],
        compiler_params=params(16),
        cost_estimate=cost(4000000000, 4 * MIB),
        name="vorticity_inside",
    )(table, flat, index)


def border_kernel(part_ref, before, after, edge, out_ref):
    rows, cols = part_ref.shape[1], before.shape[3]
    weights = ((-1.0, 9.0, -45.0), (0.0, -1.0, 9.0), (0.0, 0.0, -1.0))
    out_ref[:, 3 : rows - 3] = part_ref[:, 3 : rows - 3]
    for side in range(2):
        for r in range(3):
            halo = before if side == 0 else after
            row = r if side == 0 else rows - 1 - r
            terms = []
            for c in (1, 0):
                total = None
                for k in range(3):
                    w = weights[r][k]
                    if w != 0.0:
                        near = halo[c, k] if side == 0 else halo[c, 2 - k]
                        piece = (w if side == 0 else -w) * near
                        total = piece if total is None else total + piece
                terms.append(total)
            more = edge[0, row : row + 1, :] * terms[0] - edge[1, row : row + 1, :] * terms[1]
            for p in range(cols // 128):
                out_ref[p, row] = part_ref[p, row] + more[:, 128 * p : 128 * p + 128]


def with_border(part, before, after, edge):
    return pl.pallas_call(
        border_kernel,
        out_shape=jax.ShapeDtypeStruct(part.shape, F32),
        in_specs=[VMEM] * 4,
        out_specs=VMEM,
        compiler_params=params(8),
        cost_estimate=cost(1000000, MIB // 2),
        name="border",
    )(part, before, after, edge)


def split3(value):
    high = value.astype(BF16)
    rest = value - high.astype(F32)
    middle = rest.astype(BF16)
    low = (rest - middle.astype(F32)).astype(BF16)
    return high, middle, low


def gram_kernel(scale, copies, z_ref, parts_ref, gram_ref):
    snaps, rows = parts_ref.shape[0] // 3, z_ref.shape[1]
    total = None
    for i in range(0, rows, 2):
        for k in range(2):
            for part, value in enumerate(split3(z_ref[:, i + k].reshape(snaps, 128))):
                at = (i + k) * 128
                parts_ref[part * snaps : (part + 1) * snaps, at : at + 128] = value
        both = parts_ref[:, i * 128 : i * 128 + 256]
        dims = (((1,), (1,)), ((), ()))
        piece = lax.dot_general(both, both, dims, preferred_element_type=F32)
        total = piece if total is None else total + piece
    cut = [slice(snaps * k, snaps * (k + 1)) for k in range(3)]
    order = ((2, 2), (1, 2), (2, 1), (0, 2), (2, 0), (1, 1), (0, 1), (1, 0), (0, 0))
    gram = None
    for a, b in order:
        block = total[cut[a], cut[b]]
        gram = block if gram is None else gram + block
    gram = gram * scale
    half = snaps // 2
    tiles = []
    for block in (gram[:half, :half], gram[:half, half:], gram[half:, half:]):
        pieces = [block[8 * k : 8 * k + 8] for k in range(half // 8)]
        tiles.append(jnp.concatenate(pieces, axis=1))
    packed = jnp.concatenate(tiles, axis=0)
    for n in range(copies):
        gram_ref[n] = packed


def gram_of(z, scale, copies):
    snaps, cells = z.shape[0] * z.shape[2], z.shape[1] * z.shape[3]
    return pl.pallas_call(
        functools.partial(gram_kernel, scale, copies),
        out_shape=(
            jax.ShapeDtypeStruct((3 * snaps, cells), BF16),
            jax.ShapeDtypeStruct((copies, 24, 128), F32),
        ),
        in_specs=[VMEM],
        out_specs=(VMEM, VMEM),
        compiler_params=params(16),
        name="gram",
    )(z)


def added(values):
    total = values[0]
    for n in range(1, values.shape[0]):
        total = total + values[n]
    return total


def sum_kernel(in_ref, out_ref):
    total = added(in_ref)
    for n in range(out_ref.shape[0]):
        out_ref[n] = total


def summed(arrived, copies):
    return pl.pallas_call(
        sum_kernel,
        out_shape=jax.ShapeDtypeStruct((copies,) + arrived.shape[1:], F32),
        in_specs=[VMEM],
        out_specs=VMEM,
        compiler_params=params(4),
        name="summed",
    )(arrived)


def eliminate(rows):
    count = len(rows)
    sub = lax.broadcasted_iota(jnp.int32, (8, 128), 0)
    for b in range(count):
        cols = {
            v: [jnp.broadcast_to(rows[v][:, 8 * b + j : 8 * b + j + 1], (8, 128)) for j in range(8)]
            for v in range(b, count)
        }
        pivots = None
        for j in range(8):
            pivot = jnp.broadcast_to(cols[b][j][j : j + 1, :], (8, 128))
            pivots = pivot if pivots is None else jnp.where(sub == j, pivot, pivots)
            inverse = 1.0 / pivot
            lead = [jnp.broadcast_to(cols[b][jj][j : j + 1, :], (8, 128)) for jj in range(8)]
            lead_row = jnp.broadcast_to(rows[b][j : j + 1, :], (8, 128))
            for v in range(b, count):
                factor = cols[v][j] * inverse
                if v == b:
                    factor = jnp.where(sub > j, factor, 0.0)
                for jj in range(j + 1, 8):
                    cols[v][jj] = cols[v][jj] - factor * lead[jj]
                rows[v] = rows[v] - factor * lead_row
        root = lax.rsqrt(pivots)
        root = root * (1.5 - 0.5 * pivots * root * root)
        rows[b] = rows[b] * root
    return rows


def modes_kernel(sum_ref, parts_ref, mode_ref, operator_ref):
    snaps = parts_ref.shape[0] // 3
    half, less = snaps // 2, snaps - 1
    packed = added(sum_ref)
    lane = lax.broadcasted_iota(jnp.int32, (8, 128), 1)
    sub = lax.broadcasted_iota(jnp.int32, (8, 128), 0)
    first, cross, last = packed[:8], packed[8:16], packed[16:]

    def piece(tile, k, at):
        turn = (at - half * k) % 128
        return pltpu.roll(tile, turn, 1) if turn else tile

    fill = jnp.zeros((128 - half, 128), F32)
    cross_rows = [piece(cross, k, 0) for k in range(half // 8)]
    crossed = jnp.concatenate(cross_rows + [fill], axis=0).T
    rows = []
    for v in range(snaps // 8):
        if v < half // 8:
            block = jnp.where(lane < half, piece(first, v, 0), piece(cross, v, half))
        else:
            k = v - half // 8
            block = jnp.where(lane < half, crossed[8 * k : 8 * k + 8], piece(last, k, half))
        one = jnp.where(lane == snaps + 8 * v + sub, 1.0, 0.0)
        rows.append(jnp.where(lane < snaps, block, one))
    rows = eliminate(rows)
    couple, inverse, left = [], [], []
    for v in range(snaps // 8):
        upper = jnp.where((lane < snaps) & (lane < 8 * v + sub), 0.0, rows[v])
        turned = pltpu.roll(upper, 127, 1)
        couple.append(jnp.where(lane < less, turned, 0.0)[:, :snaps])
        turned = pltpu.roll(rows[v], 128 - snaps, 1)
        inverse.append(jnp.where(lane < less, turned, 0.0)[:, :snaps])
        turned = pltpu.roll(rows[v], 128 - snaps + 1, 1)
        left.append(jnp.where((lane > 0) & (lane < snaps), turned, 0.0)[:, :snaps])
    parts = split3(jnp.concatenate(left, axis=0))
    wide = jnp.concatenate([jnp.concatenate([part] * 3, axis=1) for part in parts], axis=0)
    for i in range(0, parts_ref.shape[1] // 128, 2):
        product = jnp.dot(wide, parts_ref[:, i * 128 : i * 128 + 256], preferred_element_type=F32)
        result = product[2 * snaps :] + product[snaps : 2 * snaps] + product[:snaps]
        for k in range(2):
            place = pl.ds(i + k, less, stride=mode_ref.shape[0] // less)
            mode_ref[place, :] = result[:less, 128 * k : 128 * k + 128]
    operator = lax.dot_general(
        jnp.concatenate(couple, axis=0),
        jnp.concatenate(inverse, axis=0),
        (((1,), (1,)), ((), ())),
        precision=lax.Precision.HIGHEST,
        preferred_element_type=F32,
    )
    operator_ref[...] = operator[:less, :less]


def modes_of(arrived, parts):
    snaps, rows = parts.shape[0] // 3, parts.shape[1] // 128
    return pl.pallas_call(
        modes_kernel,
        out_shape=(
            jax.ShapeDtypeStruct(((snaps - 1) * rows, 128), F32),
            jax.ShapeDtypeStruct((snaps - 1, snaps - 1), F32),
        ),
        in_specs=[VMEM, VMEM],
        out_specs=(VMEM, VMEM),
        compiler_params=params(16),
        name="modes",
    )(arrived, parts)


def space_groups(size):
    if size <= 8:
        return [None]
    inner = 8
    near = [[a * inner + b for b in range(inner)] for a in range(size // inner)]
    far = [[a * inner + b for a in range(size // inner)] for b in range(inner)]
    return [near, far]


def local(velocity, index, table):
    size, snap_devices = lax.axis_size("space"), lax.axis_size("snap")
    _, snaps, rows, cols = velocity.shape
    first, last = edges(velocity)
    up = [(i, i + 1) for i in range(size - 1)]
    down = [(i + 1, i) for i in range(size - 1)]
    before = lax.ppermute(last, "space", up)
    after = lax.ppermute(first, "space", down)
    flat = velocity.reshape(2, snaps * rows, cols)
    part, edge = vorticity_inside(table, flat, index)
    whole = with_border(part, before, after, edge)
    owned = lax.all_to_all(whole, "snap", 0, 0)
    all_snaps = snaps * snap_devices
    scale = 1.0 / (rows * size * cols)
    stages = [("snap", None, snap_devices)]
    for groups in space_groups(size):
        stages.append(("space", groups, size if groups is None else len(groups[0])))
    parts, sent = gram_of(owned, scale, stages[0][2])
    for n, (axis, groups, _) in enumerate(stages):
        arrived = lax.all_to_all(sent, axis, 0, 0, axis_index_groups=groups)
        if n + 1 < len(stages):
            sent = summed(arrived, stages[n + 1][2])
    mode, operator = modes_of(arrived, parts)
    return mode.reshape(all_snaps - 1, rows, 128), operator


def solution(mesh):
    in_specs = (P(None, "snap", "space", None), P("space", None), P())
    out_specs = (P(None, "space", "snap"), P())
    return jax.shard_map(local, mesh=mesh, in_specs=in_specs, out_specs=out_specs, check_vma=False)
```

```python
import functools

import jax
import jax.numpy as jnp
from jax import lax
from jax.experimental import pallas as pl
from jax.experimental.pallas import tpu as pltpu
from jax.sharding import PartitionSpec as P

F32 = jnp.float32
BF16 = jnp.bfloat16
VMEM = pl.BlockSpec(memory_space=pltpu.VMEM)
SMEM = pl.BlockSpec(memory_space=pltpu.SMEM)
HBM = pl.BlockSpec(memory_space=pltpu.HBM)
MIB = 1024 * 1024


def params(mib):
    return pltpu.CompilerParams(vmem_limit_bytes=mib * MIB)


def cost(flops, nbytes):
    return pl.CostEstimate(flops=flops, bytes_accessed=nbytes, transcendentals=0)


def edges_kernel(vel, first_ref, last_ref, head, tail, sems):
    snaps, rows = vel.shape[1], vel.shape[2]
    copies = []
    for c in range(2):
        for side, (buf, start) in enumerate(((head, 0), (tail, rows - 8))):
            src = vel.at[c, :, pl.ds(start, 8), :]
            copies.append(pltpu.make_async_copy(src, buf.at[c], sems.at[2 * c + side]))
    for copy in copies:
        copy.start()
    for c in range(2):
        for side, (buf, out) in enumerate(((head, first_ref), (tail, last_ref))):
            copies[2 * c + side].wait()
            for r in range(3):
                row = r if side == 0 else 5 + r
                for m in range(snaps):
                    out[c, r, m : m + 1, :] = buf[c, m, row : row + 1, :]


def edges(velocity):
    _, snaps, _, cols = velocity.shape
    out = jax.ShapeDtypeStruct((2, 3, snaps, cols), F32)
    return pl.pallas_call(
        edges_kernel,
        out_shape=(out, out),
        in_specs=[HBM],
        out_specs=(VMEM, VMEM),
        scratch_shapes=[
            pltpu.VMEM((2, snaps, 8, cols), F32),
            pltpu.VMEM((2, snaps, 8, cols), F32),
            pltpu.SemaphoreType.DMA((4,)),
        ],
        compiler_params=params(52),
        name="edges",
    )(velocity)


def stencil(near, middle, far):
    return 45.0 * near - 9.0 * middle + far


def metric_of(table, index):
    bits = [(index & (1 << b)) != 0 for b in range(4)]
    terms = []
    for t in range(4):
        level = [table[t, k] * (1.0 / 60.0) for k in range(16)]
        for bit in bits:
            level = [jnp.where(bit, level[2 * k + 1], level[2 * k]) for k in range(len(level) // 2)]
        terms.append(level[0])
    return terms


def band_of(line, metric, out_ref, out_first, blocks):
    lane = lax.broadcasted_iota(jnp.int32, (8, 128), 1)
    for p in range(blocks):
        span = slice(128 * p, 128 * p + 128)
        window = [[line(c, p, s) for s in range(-3, 11)] for c in range(2)]
        for s in range(8):
            total = None
            for c, xi_term, eta_term in ((1, 0, 1), (0, 2, 3)):
                near = window[c][s : s + 7]
                along = stencil(near[4] - near[2], near[5] - near[1], near[6] - near[0])
                here = near[3]
                after, before = line(c, (p + 1) % blocks, s), line(c, (p - 1) % blocks, s)
                diffs = []
                for k in (1, 2, 3):
                    ahead = pltpu.roll(jnp.where(lane < k, after, here), 128 - k, 1)
                    behind = pltpu.roll(jnp.where(lane < 128 - k, here, before), k, 1)
                    diffs.append(ahead - behind)
                around = stencil(*diffs)
                term = (
                    metric[xi_term][s : s + 1, span] * along
                    + metric[eta_term][s : s + 1, span] * around
                )
                total = term if total is None else total - term
            out_ref[p, out_first + s] = total


def turn_kernel(rows, vel, lines):
    snaps, blocks = vel.shape[1] // rows, vel.shape[2] // 128
    zero = jnp.zeros((2, blocks, 3 * snaps, 128), F32)
    lines[:, :, : 3 * snaps] = zero
    lines[:, :, (rows + 3) * snaps :] = zero
    for c in range(2):
        for m in range(snaps):
            for r in range(0, rows, 8):
                for p in range(blocks):
                    tile = vel[c, m * rows + r : m * rows + r + 8, 128 * p : 128 * p + 128]
                    lines[c, p, pl.ds((r + 3) * snaps + m, 8, stride=snaps), :] = tile


def vorticity_kernel(table, lines, index_ref, out_ref, edge_ref):
    rows, cols = index_ref.shape
    snaps, blocks = lines.shape[2] // (rows + 6), cols // 128

    def band(r, carry):
        top = 8 * r

        def line(c, p, s):
            return lines[c, p, pl.ds((top + s + 3) * snaps, snaps), :]

        metric = metric_of(table, index_ref[pl.ds(top, 8), :])
        edge_ref[0, pl.ds(top, 8), :] = metric[0]
        edge_ref[1, pl.ds(top, 8), :] = metric[2]
        band_of(line, metric, out_ref, top, blocks)
        return carry

    for r in range(rows // 8):
        band(r, 0)


def vorticity_inside(table, flat, index):
    rows, cols = index.shape
    snaps, blocks = flat.shape[1] // rows, cols // 128
    lines = pl.pallas_call(
        functools.partial(turn_kernel, rows),
        out_shape=jax.ShapeDtypeStruct((2, blocks, (rows + 6) * snaps, 128), F32),
        in_specs=[VMEM],
        out_specs=VMEM,
        compiler_params=params(16),
        cost_estimate=cost(500000000, MIB),
        name="turn",
    )(flat)
    return pl.pallas_call(
        vorticity_kernel,
        out_shape=(
            jax.ShapeDtypeStruct((blocks, rows, snaps, 128), F32),
            jax.ShapeDtypeStruct((2, rows, cols), F32),
        ),
        in_specs=[SMEM, VMEM, VMEM],
        out_specs=(VMEM, VMEM),
        compiler_params=params(16),
        cost_estimate=cost(4000000000, 4 * MIB),
        name="vorticity_inside",
    )(table, lines, index)


def border_kernel(part_ref, before, after, edge, out_ref):
    rows, cols = part_ref.shape[1], before.shape[3]
    weights = ((-1.0, 9.0, -45.0), (0.0, -1.0, 9.0), (0.0, 0.0, -1.0))
    out_ref[:, 3 : rows - 3] = part_ref[:, 3 : rows - 3]
    for side in range(2):
        for r in range(3):
            halo = before if side == 0 else after
            row = r if side == 0 else rows - 1 - r
            terms = []
            for c in (1, 0):
                total = None
                for k in range(3):
                    w = weights[r][k]
                    if w != 0.0:
                        near = halo[c, k] if side == 0 else halo[c, 2 - k]
                        piece = (w if side == 0 else -w) * near
                        total = piece if total is None else total + piece
                terms.append(total)
            more = edge[0, row : row + 1, :] * terms[0] - edge[1, row : row + 1, :] * terms[1]
            for p in range(cols // 128):
                out_ref[p, row] = part_ref[p, row] + more[:, 128 * p : 128 * p + 128]


def with_border(part, before, after, edge):
    return pl.pallas_call(
        border_kernel,
        out_shape=jax.ShapeDtypeStruct(part.shape, F32),
        in_specs=[VMEM] * 4,
        out_specs=VMEM,
        compiler_params=params(8),
        cost_estimate=cost(1000000, MIB // 2),
        name="border",
    )(part, before, after, edge)


def split3(value):
    high = value.astype(BF16)
    rest = value - high.astype(F32)
    middle = rest.astype(BF16)
    low = (rest - middle.astype(F32)).astype(BF16)
    return high, middle, low


def gram_kernel(scale, copies, z_ref, parts_ref, gram_ref):
    snaps, rows = parts_ref.shape[0] // 3, z_ref.shape[1]
    total = None
    for i in range(0, rows, 2):
        for k in range(2):
            for part, value in enumerate(split3(z_ref[:, i + k].reshape(snaps, 128))):
                at = (i + k) * 128
                parts_ref[part * snaps : (part + 1) * snaps, at : at + 128] = value
        both = parts_ref[:, i * 128 : i * 128 + 256]
        dims = (((1,), (1,)), ((), ()))
        piece = lax.dot_general(both, both, dims, preferred_element_type=F32)
        total = piece if total is None else total + piece
    cut = [slice(snaps * k, snaps * (k + 1)) for k in range(3)]
    order = ((2, 2), (1, 2), (2, 1), (0, 2), (2, 0), (1, 1), (0, 1), (1, 0), (0, 0))
    gram = None
    for a, b in order:
        block = total[cut[a], cut[b]]
        gram = block if gram is None else gram + block
    gram = gram * scale
    half = snaps // 2
    tiles = []
    for block in (gram[:half, :half], gram[:half, half:], gram[half:, half:]):
        pieces = [block[8 * k : 8 * k + 8] for k in range(half // 8)]
        tiles.append(jnp.concatenate(pieces, axis=1))
    packed = jnp.concatenate(tiles, axis=0)
    for n in range(copies):
        gram_ref[n] = packed


def gram_of(z, scale, copies):
    snaps, cells = z.shape[0] * z.shape[2], z.shape[1] * z.shape[3]
    return pl.pallas_call(
        functools.partial(gram_kernel, scale, copies),
        out_shape=(
            jax.ShapeDtypeStruct((3 * snaps, cells), BF16),
            jax.ShapeDtypeStruct((copies, 24, 128), F32),
        ),
        in_specs=[VMEM],
        out_specs=(VMEM, VMEM),
        compiler_params=params(16),
        name="gram",
    )(z)


def added(values):
    total = values[0]
    for n in range(1, values.shape[0]):
        total = total + values[n]
    return total


def sum_kernel(in_ref, out_ref):
    total = added(in_ref)
    for n in range(out_ref.shape[0]):
        out_ref[n] = total


def summed(arrived, copies):
    return pl.pallas_call(
        sum_kernel,
        out_shape=jax.ShapeDtypeStruct((copies,) + arrived.shape[1:], F32),
        in_specs=[VMEM],
        out_specs=VMEM,
        compiler_params=params(4),
        name="summed",
    )(arrived)


def eliminate(rows):
    count = len(rows)
    sub = lax.broadcasted_iota(jnp.int32, (8, 128), 0)
    for b in range(count):
        cols = {
            v: [jnp.broadcast_to(rows[v][:, 8 * b + j : 8 * b + j + 1], (8, 128)) for j in range(8)]
            for v in range(b, count)
        }
        pivots = None
        for j in range(8):
            pivot = jnp.broadcast_to(cols[b][j][j : j + 1, :], (8, 128))
            pivots = pivot if pivots is None else jnp.where(sub == j, pivot, pivots)
            inverse = 1.0 / pivot
            lead = [jnp.broadcast_to(cols[b][jj][j : j + 1, :], (8, 128)) for jj in range(8)]
            lead_row = jnp.broadcast_to(rows[b][j : j + 1, :], (8, 128))
            for v in range(b, count):
                factor = cols[v][j] * inverse
                if v == b:
                    factor = jnp.where(sub > j, factor, 0.0)
                for jj in range(j + 1, 8):
                    cols[v][jj] = cols[v][jj] - factor * lead[jj]
                rows[v] = rows[v] - factor * lead_row
        root = lax.rsqrt(pivots)
        root = root * (1.5 - 0.5 * pivots * root * root)
        rows[b] = rows[b] * root
    return rows


def modes_kernel(sum_ref, parts_ref, mode_ref, operator_ref):
    snaps = parts_ref.shape[0] // 3
    half, less = snaps // 2, snaps - 1
    packed = added(sum_ref)
    lane = lax.broadcasted_iota(jnp.int32, (8, 128), 1)
    sub = lax.broadcasted_iota(jnp.int32, (8, 128), 0)
    first, cross, last = packed[:8], packed[8:16], packed[16:]

    def piece(tile, k, at):
        turn = (at - half * k) % 128
        return pltpu.roll(tile, turn, 1) if turn else tile

    fill = jnp.zeros((128 - half, 128), F32)
    cross_rows = [piece(cross, k, 0) for k in range(half // 8)]
    crossed = jnp.concatenate(cross_rows + [fill], axis=0).T
    rows = []
    for v in range(snaps // 8):
        if v < half // 8:
            block = jnp.where(lane < half, piece(first, v, 0), piece(cross, v, half))
        else:
            k = v - half // 8
            block = jnp.where(lane < half, crossed[8 * k : 8 * k + 8], piece(last, k, half))
        one = jnp.where(lane == snaps + 8 * v + sub, 1.0, 0.0)
        rows.append(jnp.where(lane < snaps, block, one))
    rows = eliminate(rows)
    couple, inverse, left = [], [], []
    for v in range(snaps // 8):
        upper = jnp.where((lane < snaps) & (lane < 8 * v + sub), 0.0, rows[v])
        turned = pltpu.roll(upper, 127, 1)
        couple.append(jnp.where(lane < less, turned, 0.0)[:, :snaps])
        turned = pltpu.roll(rows[v], 128 - snaps, 1)
        inverse.append(jnp.where(lane < less, turned, 0.0)[:, :snaps])
        turned = pltpu.roll(rows[v], 128 - snaps + 1, 1)
        left.append(jnp.where((lane > 0) & (lane < snaps), turned, 0.0)[:, :snaps])
    parts = split3(jnp.concatenate(left, axis=0))
    wide = jnp.concatenate([jnp.concatenate([part] * 3, axis=1) for part in parts], axis=0)
    for i in range(0, parts_ref.shape[1] // 128, 2):
        product = jnp.dot(wide, parts_ref[:, i * 128 : i * 128 + 256], preferred_element_type=F32)
        result = product[2 * snaps :] + product[snaps : 2 * snaps] + product[:snaps]
        for k in range(2):
            place = pl.ds(i + k, less, stride=mode_ref.shape[0] // less)
            mode_ref[place, :] = result[:less, 128 * k : 128 * k + 128]
    operator = lax.dot_general(
        jnp.concatenate(couple, axis=0),
        jnp.concatenate(inverse, axis=0),
        (((1,), (1,)), ((), ())),
        precision=lax.Precision.HIGHEST,
        preferred_element_type=F32,
    )
    operator_ref[...] = operator[:less, :less]


def modes_of(arrived, parts):
    snaps, rows = parts.shape[0] // 3, parts.shape[1] // 128
    return pl.pallas_call(
        modes_kernel,
        out_shape=(
            jax.ShapeDtypeStruct(((snaps - 1) * rows, 128), F32),
            jax.ShapeDtypeStruct((snaps - 1, snaps - 1), F32),
        ),
        in_specs=[VMEM, VMEM],
        out_specs=(VMEM, VMEM),
        compiler_params=params(16),
        name="modes",
    )(arrived, parts)


def space_groups(size):
    if size <= 8:
        return [None]
    inner = 8
    near = [[a * inner + b for b in range(inner)] for a in range(size // inner)]
    far = [[a * inner + b for a in range(size // inner)] for b in range(inner)]
    return [near, far]


def local(velocity, index, table):
    size, snap_devices = lax.axis_size("space"), lax.axis_size("snap")
    _, snaps, rows, cols = velocity.shape
    first, last = edges(velocity)
    up = [(i, i + 1) for i in range(size - 1)]
    down = [(i + 1, i) for i in range(size - 1)]
    before = lax.ppermute(last, "space", up)
    after = lax.ppermute(first, "space", down)
    flat = velocity.reshape(2, snaps * rows, cols)
    part, edge = vorticity_inside(table, flat, index)
    whole = with_border(part, before, after, edge)
    owned = lax.all_to_all(whole, "snap", 0, 0)
    all_snaps = snaps * snap_devices
    scale = 1.0 / (rows * size * cols)
    stages = [("snap", None, snap_devices)]
    for groups in space_groups(size):
        stages.append(("space", groups, size if groups is None else len(groups[0])))
    parts, sent = gram_of(owned, scale, stages[0][2])
    for n, (axis, groups, _) in enumerate(stages):
        arrived = lax.all_to_all(sent, axis, 0, 0, axis_index_groups=groups)
        if n + 1 < len(stages):
            sent = summed(arrived, stages[n + 1][2])
    mode, operator = modes_of(arrived, parts)
    return mode.reshape(all_snaps - 1, rows, 128), operator


def solution(mesh):
    in_specs = (P(None, "snap", "space", None), P("space", None), P())
    out_specs = (P(None, "space", "snap"), P())
    return jax.shard_map(local, mesh=mesh, in_specs=in_specs, out_specs=out_specs, check_vma=False)
```
